256 devices in a mesh: dom: 64 (over x, z, core), line: 4 (over y).
Axes of the slice: x: 4, y: 4, z: 8, core: 2. Of those that a mesh axis runs over, the one named last changes fastest.
Arguments:
- right_side: float32 [64, 32768], P(None, ('dom', 'line')), may hold values from -18 to 18
- diag_blocks: bfloat16 [64, 64, 32768], P(None, None, ('dom', 'line')), may hold values from -0.5 to 3.5
- lower_blocks: bfloat16 [64, 64, 32768], P(None, None, ('dom', 'line')), may hold values from -0.375 to 0.375
- upper_blocks: bfloat16 [64, 64, 32768], P(None, None, ('dom', 'line')), may hold values from -0.375 to 0.375
- face_blocks: bfloat16 [4, 64, 64, 32768], P(None, None, None, ('dom', 'line')), may hold values from -0.75 to 0.75
- face_nbr: int32 [4, 32768], P(None, ('dom', 'line')), may hold values from 0 to 160, as said below
- send_list: int32 [2, 4096], P(None, ('dom', 'line')), may hold values from 0 to 127
- inv_blocks: bfloat16 [64, 64, 32768], P(None, None, ('dom', 'line')), may hold values from -0.75 to 0.75
- fwd_blocks: bfloat16 [64, 64, 32768], P(None, None, ('dom', 'line')), may hold values from -0.625 to 0.625
- bwd_blocks: bfloat16 [64, 64, 32768], P(None, None, ('dom', 'line')), may hold values from -0.625 to 0.625
Outputs:
- update: float32 [64, 32768], P(None, ('dom', 'line'))
- hessenberg: float32 [4, 3], replicated
The draws below stay inside these ranges and needn't reach their ends.
Inputs may be any that keep to these rules, and one draw needn't show every extreme that they name: `face_nbr`: slots 128 to 159 name values received from the neighbouring partitions and slot 160 is the zero slot.
All inputs are finite; a program needn't handle non-finite values.
Results may differ from the reference program's by a relative error of at most 0.015.
Values may be sent and summed in bfloat16 or wider, within the bound.
A program may use at most 64 MiB of HBM per device.

```python
import jax
import jax.numpy as jnp
from jax import lax

B = 64
LLEN = 32
FACES = 4
HALO = 16
ITERS = 3
LINES_DEV = 16
ELOC = 128
ELEMS = 32768
N_DOM = 64
N_LINE = 4


def draw_right_side(key, part):
    spread = jnp.arange(ELEMS, dtype=jnp.float32) / ELEMS
    scale = 1.0 + 2.0 * spread
    jitter = jnp.clip(jax.random.normal(key, (B, ELEMS), jnp.float32), -6.0, 6.0)
    return (jitter * scale[None, :]).astype(jnp.float32)


def draw_diag_blocks(key, part):
    first_key, second_key = jax.random.split(jax.random.fold_in(key, 11))
    leading = jax.random.uniform(first_key, (B, ELEMS), jnp.float32, 1.5, 3.0)
    jitter = jnp.clip(0.125 * jax.random.normal(second_key, (B, B, ELEMS), jnp.float32), -0.5, 0.5)
    blocks = jitter + jnp.eye(B, dtype=jnp.float32)[:, :, None] * leading[:, None, :]
    return blocks.astype(jnp.bfloat16)


def draw_face_nbr(key, part):
    base_key = jax.random.fold_in(key, 23)
    left_key = jax.random.fold_in(base_key, 0)
    right_key = jax.random.fold_in(base_key, 1)
    pick_key = jax.random.fold_in(base_key, 2)
    rest_key = jax.random.fold_in(base_key, 4)
    from_left = ELOC + jax.random.randint(left_key, (ELEMS,), 0, HALO)
    from_right = ELOC + HALO + jax.random.randint(right_key, (ELEMS,), 0, HALO)
    either_side = ELOC + jax.random.randint(pick_key, (ELEMS,), 0, 2 * HALO)
    rows = [from_left, from_right, either_side]
    for face in range(3, FACES):
        rows.append(jax.random.randint(jax.random.fold_in(rest_key, face), (ELEMS,), 0, ELOC + 2 * HALO + 1))
    table = jnp.stack(rows[:FACES], axis=0).astype(jnp.int32)
    table = table.at[FACES - 1, 0].set(ELOC + 2 * HALO)
    return table.astype(jnp.int32)


def plant(entries, key, smallest, largest):
    longest = entries.shape.index(max(entries.shape))
    spots = []
    for shift in (0, 1):
        where = [jax.random.randint(jax.random.fold_in(key, axis), (), 0, length) for axis, length in enumerate(entries.shape)]
        where[longest] = (where[longest] + shift) % entries.shape[longest]
        spots.append(tuple(where))
    return entries.at[spots[0]].set(smallest).at[spots[1]].set(largest)


def block_levels(rng, dims, pieces, smallest, top_value):
    def one(axis_at, blocks):
        steps = jax.random.uniform(jax.random.fold_in(jax.random.fold_in(rng, 6), axis_at), (blocks,), jnp.float32, smallest / len(pieces), top_value / len(pieces))
        return jnp.repeat(jnp.exp(steps), dims[axis_at] // blocks).reshape((-1,) + (1,) * (len(dims) - axis_at - 1))

    gain = one(*pieces[0])
    for cut in pieces[1:]:
        gain = gain * one(*cut)
    return gain


def normal_values(stream_key, shape, scale, most, cuts=(), kind=jnp.bfloat16):
    loudness = block_levels(stream_key, shape, cuts, -0.22, 0.18) if cuts else 1.0
    entries = jax.random.normal(stream_key, shape, jnp.float32) * scale * loudness
    return jnp.minimum(jnp.maximum(entries, -most), most).astype(kind)


def setup_inputs(seed: int = 0) -> dict:
    splits = jax.random.split(jax.random.key(seed), 11)
    return {
        "right_side": draw_right_side(jax.random.fold_in(splits[10], 71), 0),
        "diag_blocks": draw_diag_blocks(jax.random.fold_in(splits[10], 71), 0),
        "lower_blocks": normal_values(splits[2], (B, B, ELEMS), (4 * B) ** -0.5, 0.375, ((2, 256),)),
        "upper_blocks": normal_values(splits[3], (B, B, ELEMS), (4 * B) ** -0.5, 0.375, ((2, 256),)),
        "face_blocks": normal_values(splits[4], (FACES, B, B, ELEMS), B ** -0.5, 0.75, ((3, 256),)),
        "face_nbr": draw_face_nbr(jax.random.fold_in(splits[10], 71), 0),
        "send_list": plant(jax.random.randint(splits[6], (2, HALO * N_DOM * N_LINE), 0, ELOC), jax.random.fold_in(splits[6], 1), 0, ELOC - 1).astype(jnp.int32),
        "inv_blocks": normal_values(splits[7], (B, B, ELEMS), B ** -0.5, 0.75, ((2, 256),)),
        "fwd_blocks": normal_values(splits[8], (B, B, ELEMS), (B * 7 // 5) ** -0.5, 0.625, ((2, 256),)),
        "bwd_blocks": normal_values(splits[9], (B, B, ELEMS), (B * 7 // 5) ** -0.5, 0.625, ((2, 256),)),
    }


HIGHEST = lax.Precision.HIGHEST

def apply_blocks(blocks, rounded):
    return jnp.einsum('ije,je->ie', blocks.astype(jnp.float32), rounded.astype(jnp.float32), precision=HIGHEST)

def couple(blocks, carried):
    return jnp.einsum('ijnl,jnl->inl', blocks.astype(jnp.float32), carried, precision=HIGHEST)

def operate(vector, diag_blocks, lower_blocks, upper_blocks, face_blocks, face_nbr, send_list):
    rounded = vector.astype(jnp.bfloat16)
    summed = apply_blocks(diag_blocks, rounded)
    gridded = rounded.reshape(B, N_DOM, LLEN, LINES_DEV)
    earlier = jnp.pad(gridded, ((0, 0), (0, 0), (1, 0), (0, 0)))[:, :, :-1]
    following = jnp.pad(gridded, ((0, 0), (0, 0), (0, 1), (0, 0)))[:, :, 1:]
    summed = summed + apply_blocks(lower_blocks, earlier.reshape(B, ELEMS))
    summed = summed + apply_blocks(upper_blocks, following.reshape(B, ELEMS))
    partition = rounded.reshape(B, N_DOM, N_LINE, ELOC)
    sending = send_list.reshape(2, N_DOM, N_LINE, HALO)
    to_right = jnp.take_along_axis(partition, sending[0][None], axis=3)
    to_left = jnp.take_along_axis(partition, sending[1][None], axis=3)
    from_left = jnp.pad(to_right, ((0, 0), (1, 0), (0, 0), (0, 0)))[:, :-1]
    from_right = jnp.pad(to_left, ((0, 0), (0, 1), (0, 0), (0, 0)))[:, 1:]
    empty_slot = jnp.zeros((B, N_DOM, N_LINE, 1), jnp.bfloat16)
    extended = jnp.concatenate([partition, from_left, from_right, empty_slot], axis=3)
    slots = face_nbr.reshape(FACES, N_DOM, N_LINE, ELOC)
    for face in range(FACES):
        picked = jnp.take_along_axis(extended, slots[face][None], axis=3)
        summed = summed + apply_blocks(face_blocks[face], picked.reshape(B, ELEMS))
    return summed

def precondition(vector, inv_blocks, fwd_blocks, bwd_blocks):
    source = apply_blocks(inv_blocks, vector.astype(jnp.bfloat16)).reshape(B, N_DOM, LLEN, LINES_DEV)
    forward_couple = fwd_blocks.reshape(B, B, N_DOM, LLEN, LINES_DEV)
    backward_couple = bwd_blocks.reshape(B, B, N_DOM, LLEN, LINES_DEV)
    carried = jnp.zeros((B, N_DOM, LINES_DEV), jnp.float32)
    forward = []
    for position in range(LLEN):
        carried = source[:, :, position] - couple(forward_couple[:, :, :, position], carried)
        forward.append(carried)
    carried = jnp.zeros((B, N_DOM, LINES_DEV), jnp.float32)
    backward = [None] * LLEN
    for position in reversed(range(LLEN)):
        carried = forward[position] - couple(backward_couple[:, :, :, position], carried)
        backward[position] = carried
    return jnp.stack(backward, axis=2).reshape(B, ELEMS)

def reference(right_side, diag_blocks, lower_blocks, upper_blocks, face_blocks, face_nbr, send_list, inv_blocks, fwd_blocks, bwd_blocks):
    start_norm = jnp.sqrt(jnp.sum(right_side * right_side))
    krylov = [right_side / start_norm]
    search = []
    hessenberg = jnp.zeros((ITERS + 1, ITERS), jnp.float32)
    for iteration in range(ITERS):
        direction = precondition(krylov[iteration], inv_blocks, fwd_blocks, bwd_blocks)
        search.append(direction)
        product_vec = operate(direction, diag_blocks, lower_blocks, upper_blocks, face_blocks, face_nbr, send_list)
        for column in range(iteration + 1):
            weight_ij = jnp.sum(product_vec * krylov[column])
            product_vec = product_vec - weight_ij * krylov[column]
            hessenberg = hessenberg.at[column, iteration].set(weight_ij)
        height = jnp.sqrt(jnp.sum(product_vec * product_vec))
        hessenberg = hessenberg.at[iteration + 1, iteration].set(height)
        if iteration + 1 < ITERS:
            krylov.append(product_vec / height)
    normal = jnp.dot(hessenberg.T, hessenberg, precision=HIGHEST)
    target = start_norm * hessenberg[0]
    factor = jnp.linalg.cholesky(normal)
    coeffs = jax.scipy.linalg.cho_solve((factor, True), target)
    update = coeffs[0] * search[0]
    for iteration in range(1, ITERS):
        update = update + coeffs[iteration] * search[iteration]
    return (update, hessenberg)
```

```python
import functools

import jax
import jax.numpy as jnp
from jax import lax
from jax.experimental import pallas as pl
from jax.experimental.pallas import tpu as pltpu
from jax.sharding import PartitionSpec as P

MESH = pl.DeviceIdType.MESH
F32 = jnp.float32
BF16 = jnp.bfloat16
ITERS = 3
B = 64
E = 128
LINES = 16
Q = 8
HALF = Q // 2
HALO = 16
FACES = 4
START_SCALE = 2.0**-15
W_SCALE = 2.0**-24


def iota(shape, dim):
    return lax.broadcasted_iota(jnp.int32, shape, dim)


def merge_rows(parts):
    sub = iota((8, E), 0)

    def keeps(shift, bases):
        mask = sub == bases[0]
        for base in bases[1:]:
            mask = mask | (sub == base)
        return mask

    def join(a, b, roll, mask_a):
        sel_here = jnp.where(mask_a, a, b)
        shifted = keepers[id(mask_a)]
        sel_there = jnp.where(shifted, a, b)
        return sel_here + pltpu.roll(sel_there, roll, 0)

    keepers = {}

    def level(mask_rows, roll):
        mask = keeps(roll, mask_rows)
        moved = keeps(roll, [(row - roll) % 8 for row in mask_rows])
        keepers[id(mask)] = moved
        return mask

    out = {}

    def quad(lo, hi, first):
        rows = [(first + r) % 8 for r in range(4)]
        return join(parts[lo], parts[hi], 4, masks4[first % 8])

    masks4 = {f: level([(f + r) % 8 for r in range(4)], 4) for f in (0, 6, 7, 5)}
    mask_23 = level([2, 3, 6, 7], 2)
    d_odd = join(quad(3, 7, 0), quad(1, 5, 6), 2, mask_23)
    mask_12 = level([1, 2, 5, 6], 2)
    d_even = join(quad(2, 6, 7), quad(0, 4, 5), 2, mask_12)
    mask_odd = level([1, 3, 5, 7], 1)
    return join(d_odd, d_even, 1, mask_odd)


def fold(array):
    groups = [array[8 * r : 8 * r + 8] for r in range(8)]
    while len(groups) > 1:
        groups = [a + b for a, b in zip(groups[::2], groups[1::2])]
    return groups[0]


def kernel(
    sizes,
    right_hbm,
    nbr_hbm,
    send_hbm,
    diag_hbm,
    lower_hbm,
    upper_hbm,
    face_hbm,
    inv_hbm,
    fwd_hbm,
    bwd_hbm,
    update_ref,
    hess_ref,
    right_ref,
    nbr_ref,
    send_ref,
    diag,
    lower,
    upper,
    face,
    inv,
    fwd,
    bwd,
    turned,
    prefix_map,
    chunk_map,
    both_map,
    got_map,
    inflow_map,
    pick,
    send_pick,
    lists,
    vecs,
    source,
    state,
    keep,
    ends,
    got_ends,
    halo_out,
    got_halo,
    part,
    got_a,
    got_b,
    load_sem,
    map_send,
    map_recv,
    end_send,
    end_recv,
    halo_send,
    halo_recv,
    sum_send,
    sum_recv,
):
    n_dom, n_line, high, low = sizes
    n_a, n_b = n_line * high, low
    dom = lax.axis_index("dom")
    line = lax.axis_index("line")
    dom_high = dom // low
    dom_low = dom % low
    place_a = line * high + dom_high

    loads = []
    for slot, (src, dst) in enumerate(
        (
            (fwd_hbm, fwd),
            (bwd_hbm, bwd),
            (right_hbm, right_ref),
            (nbr_hbm, nbr_ref),
            (send_hbm, send_ref),
            (inv_hbm, inv),
            (diag_hbm, diag),
            (upper_hbm, upper),
            (lower_hbm, lower),
            (face_hbm, face),
        )
    ):
        copy = pltpu.make_async_copy(src, dst, load_sem.at[slot])
        copy.start()
        loads.append(copy)

    def around(count, off):
        return min(off, count - off)

    def offsets(first, second):
        pairs = [(a, b) for a in range(first) for b in range(second) if a or b]
        return sorted(pairs, key=lambda p: -around(first, p[0]) - around(second, p[1]))

    peers_a = [
        {"dom": (dom_high + b) % high * low + dom_low, "line": (line + a) % n_line} for a, b in offsets(n_line, high)
    ]
    pairs = low // 2
    peers_b = [
        {"dom": dom_high * low + (dom_low // 2 + a) % pairs * 2 + (dom_low % 2 + b) % 2, "line": line}
        for a, b in offsets(pairs, 2)
    ]

    def peer_line(off):
        return {"dom": dom, "line": (line + off + n_line) % n_line}

    def peer_dom(off):
        return {"dom": (dom + off + n_dom) % n_dom, "line": line}

    inflow_map[...] = jnp.zeros_like(inflow_map)

    barrier = pltpu.get_barrier_semaphore()
    partners = peers_a + peers_b + [peer_dom(1), peer_dom(-1)]
    for partner in partners:
        pl.semaphore_signal(barrier, inc=1, device_id=partner, device_id_type=MESH)

    lane = iota((B, E), 1)
    lane8 = iota((8, E), 1)
    position = lane // LINES

    pending = []

    def sum_start(which, rows):
        rows = list(rows) + [jnp.zeros((8, E), F32)] * (8 - len(rows))
        part[which] = merge_rows(rows)
        got_a[which, place_a] = part[which]
        for peer in peers_a:
            pltpu.make_async_remote_copy(
                src_ref=part.at[which],
                dst_ref=got_a.at[which, place_a],
                send_sem=sum_send.at[which],
                recv_sem=sum_recv.at[which],
                device_id=peer,
                device_id_type=MESH,
            ).start()

    def whole_wait(ref, sem):
        pltpu.make_async_copy(ref, ref, sem).wait()

    def sum_middle(which):
        whole_wait(got_a.at[which, pl.ds(0, n_a - 1)], sum_recv.at[which])
        total = got_a[which, 0]
        for slot in range(1, n_a):
            total = total + got_a[which, slot]
        part[4 + which] = total
        got_b[which, dom_low] = total
        for peer in peers_b:
            pltpu.make_async_remote_copy(
                src_ref=part.at[4 + which],
                dst_ref=got_b.at[which, dom_low],
                send_sem=sum_send.at[4 + which],
                recv_sem=sum_recv.at[4 + which],
                device_id=peer,
                device_id_type=MESH,
            ).start()

    def sum_end(which):
        whole_wait(got_b.at[which, pl.ds(0, n_b - 1)], sum_recv.at[4 + which])
        total = got_b[which, 0]
        for slot in range(1, n_b):
            total = total + got_b[which, slot]
        sums = jnp.sum(total, axis=1, keepdims=True)
        return [sums[row : row + 1, :] for row in range(8)]

    def block_pass(blocks, vectors, emit):
        def body(group, _):
            sums = [None] * 8
            for block, vector in zip(blocks, vectors):
                values = vector[...]
                for row in range(8):
                    got = fold(block(group * 8 + row).astype(F32) * values)
                    sums[row] = got if sums[row] is None else sums[row] + got
            emit(pl.ds(pl.multiple_of(group * 8, 8), 8), merge_rows(sums))
            return 0

        lax.fori_loop(0, B // 8, body, 0, unroll=len(blocks) == 1)

    def spread(array, at):
        array = jnp.where(position == at, array, 0.0)
        for step in (LINES, 2 * LINES, 4 * LINES):
            array = array + pltpu.roll(array, step, 1)
        return array

    line_mask = [jnp.where(lane % LINES == m, 1.0, 0.0).astype(BF16) for m in range(LINES)]

    def stacked(vector):
        upper_half = vector.astype(BF16)
        lower_half = (vector - upper_half.astype(F32)).astype(BF16)
        halves = [jnp.concatenate([half * mask for mask in line_mask], axis=0) for half in (upper_half, lower_half)]
        return jnp.concatenate(halves, axis=1)

    def apply_maps(maps, vectors):
        right = jnp.concatenate([stacked(vector) for vector in vectors], axis=0)
        both = jnp.dot(maps, right, preferred_element_type=F32)
        return both[:, :E] + both[:, E:]

    def place(base, rows, steps, way):
        total = jnp.zeros((B, E), F32)
        for index, step in enumerate(steps):
            at = step if way == 0 else Q - 1 - step
            total = jnp.where(position == at, rows[index * B : index * B + B], total)
        return base + total

    def pack(array):
        total = array[0:8]
        for row in range(1, 8):
            total = jnp.where(lane8 // LINES == row, array[8 * row : 8 * row + 8], total)
        return total

    row_group = iota((B, E), 0) // 8

    def unpack(array):
        array = jnp.where(position == row_group, jnp.concatenate([array] * 8, axis=0), 0.0)
        for step in (LINES, 2 * LINES, 4 * LINES):
            array = array + pltpu.roll(array, step, 1)
        return array

    row32 = iota((32, E), 0)
    lane32 = iota((32, E), 1)
    selector = jnp.where(lane32 // 4 == row32, 1.0, 0.0).astype(BF16)
    quarter = [jnp.where(lane % 4 == m, 1.0, 0.0).astype(BF16) for m in range(4)]
    column_part = iota((B, 256), 1) // B
    column_mask = [jnp.where(column_part == m, 1.0, 0.0).astype(BF16) for m in range(4)]

    def turn(blocks):
        def body(i, _):
            rows = blocks[i]
            stack = jnp.concatenate([rows * quarter[m] for m in range(4)], axis=0)
            got = lax.dot_general(selector, stack, (((1,), (1,)), ((), ())), preferred_element_type=F32)
            turned[0, pl.ds(i, 32, stride=B), :] = got[:, :E]
            turned[1, pl.ds(i, 32, stride=B), :] = got[:, E:]
            return 0

        lax.fori_loop(0, B, body, 0, unroll=16)

    def matrix(way, step, group):
        at = step if way == 0 else Q - 1 - step
        rows = pl.ds((at * 4 + group) * B, B)
        return jnp.concatenate([turned[0, rows, :], turned[1, rows, :]], axis=1)

    def diagonal(array):
        return jnp.concatenate([array * column_mask[m] for m in range(4)], axis=0)

    def columns(group):
        return pl.ds(group * 256, 256)

    def build(way):
        for group in range(4):
            first = [None] * HALF
            second = [None] * HALF
            for step in range(HALF):
                for store, at in ((first, step), (second, HALF + step)):
                    mine = matrix(way, at, group)
                    if step == 0:
                        store[step] = (-mine).astype(BF16)
                    else:
                        store[step] = -jnp.dot(
                            mine.astype(BF16), diagonal(store[step - 1]), preferred_element_type=F32
                        )
                        store[step] = store[step].astype(BF16)
            for step in range(HALF):
                prefix_map[way, step * B : step * B + B, columns(group)] = first[step]
                chunk_map[way, step * B : step * B + B, columns(group)] = second[step]
            later = jnp.dot(chunk_map[way, :, columns(group)], diagonal(first[-1]), preferred_element_type=F32)
            prefix_map[way, HALF * B :, columns(group)] = later.astype(BF16)

    def build_both():
        for group in range(4):
            last = prefix_map[0, (Q - 1) * B :, columns(group)]
            both_map[(Q - 1) * B :, columns(group)] = last
            for at in reversed(range(Q - 1)):
                got = jnp.dot(
                    matrix(1, Q - 1 - at, group).astype(BF16), diagonal(last), preferred_element_type=F32
                )
                last = (prefix_map[0, at * B : at * B + B, columns(group)].astype(F32) - got).astype(BF16)
                both_map[at * B : at * B + B, columns(group)] = last

    def sweep(blocks, way):
        starts = position % HALF == (0 if way == 0 else HALF - 1)
        shift = LINES if way == 0 else E - LINES
        base = source[...]
        now = base
        for _ in range(HALF - 1):
            vecs[0] = jnp.where(starts, 0.0, pltpu.roll(now, shift, 1))

            def emit(rows, got):
                state[rows, :] = source[rows, :] - got

            block_pass([lambda i: blocks[i]], [vecs.at[0]], emit)
            now = state[...]
        last = HALF - 1 if way == 0 else HALF
        inflow = spread(now, last)
        end_rows = apply_maps(chunk_map[way, (HALF - 1) * B :, :], [inflow])
        end = spread(now, Q - 1 if way == 0 else 0) + end_rows

        def finish():
            rows = apply_maps(chunk_map[way, : (HALF - 1) * B, :], [inflow])
            whole = place(now, rows, range(HALF, Q - 1), way)
            return place(whole, end_rows, [Q - 1], way)

        return end, finish

    def exchange_start(index, way, end):
        ends[index] = pack(end)
        copies = {}
        for away in sorted(range(1, n_line), key=lambda n: -around(n_line, n)):
            copy = pltpu.make_async_remote_copy(
                src_ref=ends.at[index],
                dst_ref=got_ends.at[index, away - 1],
                send_sem=end_send.at[index, away - 1],
                recv_sem=end_recv.at[index, away - 1],
                device_id=peer_line(away if way == 0 else -away),
                device_id_type=MESH,
            )
            copy.start()
            copies[away] = copy
        return copies

    def entering(index, way, copies):
        room = line if way == 0 else n_line - 1 - line
        got = []
        for away in range(1, n_line):
            copies[away].wait_recv()
            got.append(unpack(jnp.where(room >= away, got_ends[index, away - 1], 0.0)))
        return got[0] + apply_maps(inflow_map[way], got[1:3])

    sent = []

    def precondition(iteration, after_send, after_solve):
        def emit(rows, got):
            source[rows, :] = got

        block_pass([lambda i: inv[i]], [vecs.at[0]], emit)
        end, finish = sweep(fwd, 0)
        copies = exchange_start(2 * iteration, 0, end)
        sent.extend(copies.values())
        values = finish()
        if iteration == 0:
            after_send()
            inflow = entering(0, 0, copies)
            source[...] = place(values, apply_maps(prefix_map[0], [inflow]), range(Q), 0)
            end, finish = sweep(bwd, 1)
            copies = exchange_start(1, 1, end)
            sent.extend(copies.values())
            values = finish()
            after_solve()
        else:
            source[...] = values
            end, finish = sweep(bwd, 1)
            values = finish()
            after_send()
            inflow = entering(2 * iteration, 0, copies)
            end = end + apply_maps(both_map[:B, :], [inflow])
            copies = exchange_start(2 * iteration + 1, 1, end)
            sent.extend(copies.values())
            values = place(values, apply_maps(both_map[...], [inflow]), range(Q), 0)
            after_solve()
        inflow = entering(2 * iteration + 1, 1, copies)
        return place(values, apply_maps(prefix_map[1], [inflow]), range(Q), 1), inflow

    def operate(iteration, values, inflow):
        rounded = values.astype(BF16)
        halo_out[iteration] = jnp.dot(rounded, send_pick[...], preferred_element_type=F32).astype(BF16)
        copies = []
        for slot, peer in enumerate((peer_dom(1), peer_dom(-1), peer_line(1))):
            copy = pltpu.make_async_remote_copy(
                src_ref=halo_out.at[iteration],
                dst_ref=got_halo.at[iteration, slot],
                send_sem=halo_send.at[iteration, slot],
                recv_sem=halo_recv.at[iteration, slot],
                device_id=peer,
                device_id_type=MESH,
            )
            copy.start()
            copies.append(copy)
        sent.extend(copies)
        vecs[0] = values
        vecs[1] = pltpu.roll(jnp.where(position == 0, inflow, values), E - LINES, 1)

        def emit_first(rows, got):
            state[rows, :] = got

        block_pass([lambda i: diag[i], lambda i: upper[i]], [vecs.at[0], vecs.at[1]], emit_first)
        rest = (values - rounded.astype(F32)).astype(BF16)
        here = jnp.dot(jnp.concatenate([rounded, rest], axis=0), pick[:E, :], preferred_element_type=F32)
        copies[2].wait_recv()
        behind = jnp.where(line > 0, got_halo[iteration, 2].astype(F32), 0.0)
        vecs[2] = pltpu.roll(jnp.where(position == Q - 1, behind, values), LINES, 1)

        def emit_more(rows, got):
            state[rows, :] = state[rows, :] + got

        block_pass([lambda i: lower[i]], [vecs.at[2]], emit_more)
        copies[0].wait_recv()
        copies[1].wait_recv()
        left = jnp.where(dom > 0, got_halo[iteration, 0].astype(F32), 0.0)
        right = jnp.where(dom < n_dom - 1, got_halo[iteration, 1].astype(F32), 0.0)
        received = jnp.where(lane < HALO, left, jnp.where(lane < 2 * HALO, right, 0.0)).astype(BF16)
        picked = here[:B] + here[B:] + jnp.dot(received, pick[E:, :], preferred_element_type=F32)
        for side in range(FACES):
            vecs[3 + side] = picked[:, side * E : side * E + E]

        def emit_second(rows, got):
            keep[6, rows, :] = state[rows, :] + got

        block_pass(
            [lambda i, side=side: face[side, i] for side in range(FACES)],
            [vecs.at[3 + side] for side in range(FACES)],
            emit_second,
        )

    loads[0].wait()
    turn(fwd)
    build(0)

    pl.semaphore_wait(barrier, len(partners))
    def rooms(way):
        return line if way == 0 else n_line - 1 - line

    def map_copy(way, away):
        return pltpu.make_async_remote_copy(
            src_ref=prefix_map.at[way, pl.ds((Q - 1) * B, B), :],
            dst_ref=got_map.at[way] if away == 2 else inflow_map.at[way, :, pl.ds(0, LINES * B)],
            send_sem=map_send.at[way, away - 1],
            recv_sem=map_recv.at[way, away - 1],
            device_id=peer_line(away if way == 0 else -away),
            device_id_type=MESH,
        )

    def sends_map(way, away):
        return (rooms(way) >= 1) & (rooms(way) + away < n_line)

    def send_maps(way):
        for away in (1, 2):

            @pl.when(sends_map(way, away))
            def _():
                map_copy(way, away).start()

    send_maps(0)
    loads[2].wait()
    vector = right_ref[...] * START_SCALE
    keep[3] = vector
    sum_start(0, [fold(vector * vector)])

    loads[3].wait()
    loads[4].wait()
    for side in range(FACES):
        hit = iota((256, E), 0) == nbr_ref[side : side + 1, :]
        pick[:, side * E : side * E + E] = jnp.where(hit, 1.0, 0.0).astype(BF16)
    lists[...] = jnp.zeros((8, E), jnp.int32)
    lists[0:1, 0:HALO] = send_ref[0:1, :]
    lists[1:2, 0:HALO] = send_ref[1:2, :]
    now = lists[...]
    moved = pltpu.roll(now, HALO, 1)
    lane_row = lane8[0:1]
    wanted = jnp.where(
        lane_row < HALO,
        now[0:1],
        jnp.where(lane_row < 2 * HALO, moved[1:2], jnp.where(lane_row >= (Q - 1) * LINES, lane_row, -1)),
    )
    send_pick[...] = jnp.where(iota((E, E), 0) == wanted, 1.0, 0.0).astype(BF16)

    loads[5].wait()

    def first_after_send():
        loads[1].wait()
        turn(bwd)
        build(1)
        send_maps(1)
        join_maps(0)
        sum_middle(0)

    def first_after_solve():
        build_both()
        join_maps(1)

    def join_maps(way):
        @pl.when(rooms(way) >= 2)
        def _():
            map_copy(way, 1).wait_recv()

        @pl.when(rooms(way) >= 3)
        def _():
            map_copy(way, 2).wait_recv()
            for group in range(4):
                near = inflow_map[way, :, columns(group)]
                both = jnp.dot(near, diagonal(got_map[way, :, columns(group)]), preferred_element_type=F32)
                inflow_map[way, :, columns(4 + group)] = both.astype(BF16)

    vecs[0] = vector
    values, inflow = precondition(0, first_after_send, first_after_solve)
    norm = jnp.sqrt(sum_end(0)[0])
    start_norm = norm * (1.0 / START_SCALE)
    search = values / norm
    keep[0] = search
    keep[3] = keep[3] / norm
    keep[7] = inflow / norm
    for slot in range(6, 10):
        loads[slot].wait()
    operate(0, search, keep[7])
    w = keep[6]
    first = keep[3]
    sum_start(1, [fold(w * first), fold(w * w)])

    vecs[0] = w * W_SCALE
    values, inflow = precondition(1, lambda: sum_middle(1), lambda: None)
    s = sum_end(1)
    tiny = 1e-14
    h11 = s[0]
    g1 = jnp.sqrt(jnp.maximum(s[1] - h11 * h11, tiny * s[1]))
    turn_back = 1.0 / W_SCALE
    first = keep[3]
    second = (keep[6] - h11 * first) / g1
    keep[4] = second
    search = (values / g1) * turn_back - (h11 / g1) * keep[0]
    entry = (inflow / g1) * turn_back - (h11 / g1) * keep[7]
    keep[1] = search
    keep[8] = entry
    operate(1, search, entry)
    w = keep[6]
    first = keep[3]
    second = keep[4]
    sum_start(2, [fold(w * first), fold(w * second), fold(w * w), fold(first * second), fold(second * second)])

    vecs[0] = w * W_SCALE
    values, inflow = precondition(2, lambda: sum_middle(2), lambda: None)
    s = sum_end(2)
    size2 = jnp.sqrt(s[4])
    h21 = g1 * size2
    h12 = s[0] / size2
    cross12 = s[3] / size2
    along2 = s[1] / (size2 * size2)
    h22 = along2 - h12 * cross12
    all2 = s[2] / (size2 * size2)
    rest2 = all2 + h12 * h12 + h22 * h22 - 2.0 * h12 * h12 - 2.0 * h22 * along2 + 2.0 * h12 * h22 * cross12
    g2 = jnp.sqrt(jnp.maximum(rest2, tiny * all2))
    from_w = 1.0 / (size2 * g2)
    from_1 = h12 / g2
    from_2 = h22 / (size2 * g2)
    third = from_w * keep[6] - from_1 * keep[3] - from_2 * keep[4]
    keep[5] = third
    search = (from_w * values) * turn_back - from_1 * keep[0] - from_2 * keep[1]
    entry = (from_w * inflow) * turn_back - from_1 * keep[7] - from_2 * keep[8]
    keep[2] = search
    operate(2, search, entry)
    w = keep[6]
    first = keep[3]
    second = keep[4]
    third = keep[5]
    sum_start(
        3,
        [
            fold(w * first),
            fold(w * second),
            fold(w * third),
            fold(w * w),
            fold(first * third),
            fold(second * third),
            fold(third * third),
        ],
    )
    sum_middle(3)
    s = sum_end(3)
    size3 = jnp.sqrt(s[6])
    h32 = g2 * size3
    h13 = s[0] / size3
    along2 = s[1] / (size3 * size2)
    along3 = s[2] / (size3 * size3)
    all3 = s[3] / (size3 * size3)
    cross13 = s[4] / size3
    cross23 = s[5] / (size3 * size2)
    h23 = along2 - h13 * cross12
    h33 = along3 - h13 * cross13 - h23 * cross23
    rest3 = (
        all3
        + h13 * h13
        + h23 * h23
        + h33 * h33
        - 2.0 * (h13 * h13 + h23 * along2 + h33 * along3)
        + 2.0 * (h13 * h23 * cross12 + h13 * h33 * cross13 + h23 * h33 * cross23)
    )
    h43 = jnp.sqrt(jnp.maximum(rest3, 0.0))

    n11 = h11 * h11 + h21 * h21
    n21 = h11 * h12 + h21 * h22
    n31 = h11 * h13 + h21 * h23
    n22 = h12 * h12 + h22 * h22 + h32 * h32
    n32 = h12 * h13 + h22 * h23 + h32 * h33
    n33 = h13 * h13 + h23 * h23 + h33 * h33 + h43 * h43
    l11 = jnp.sqrt(n11)
    l21 = n21 / l11
    l31 = n31 / l11
    l22 = jnp.sqrt(n22 - l21 * l21)
    l32 = (n32 - l31 * l21) / l22
    l33 = jnp.sqrt(n33 - l31 * l31 - l32 * l32)
    f1 = start_norm * h11 / l11
    f2 = (start_norm * h12 - l21 * f1) / l22
    f3 = (start_norm * h13 - l31 * f1 - l32 * f2) / l33
    c3 = f3 / l33
    c2 = (f2 - l32 * c3) / l22
    c1 = (f1 - l21 * c2 - l31 * c3) / l11
    update_ref[...] = c1 * keep[0] + (c2 / size2) * keep[1] + (c3 / size3) * keep[2]
    entries = {
        (0, 0): h11,
        (1, 0): h21,
        (0, 1): h12,
        (1, 1): h22,
        (2, 1): h32,
        (0, 2): h13,
        (1, 2): h23,
        (2, 2): h33,
        (3, 2): h43,
    }
    table = jnp.zeros((8, E), F32)
    sub8 = iota((8, E), 0)
    for (row, column), value in entries.items():
        table = jnp.where((sub8 == row) & (lane8 == column), value, table)
    hess_ref[...] = table[0 : ITERS + 1, 0:ITERS]

    for copy in sent:
        copy.wait_send()
    for way in range(2):
        for away in (1, 2):

            @pl.when(sends_map(way, away))
            def _():
                map_copy(way, away).wait_send()

    for which in range(4):
        whole_wait(got_a.at[which, pl.ds(0, n_a - 1)], sum_send.at[which])
        whole_wait(got_b.at[which, pl.ds(0, n_b - 1)], sum_send.at[4 + which])


def shards(sizes, right_side, diag, lower, upper, face, nbr, send, inv, fwd, bwd):
    n_dom, n_line, high, low = sizes
    n_a, n_b = n_line * high, low
    vmem = pl.BlockSpec(memory_space=pltpu.VMEM)
    hbm = pl.BlockSpec(memory_space=pltpu.HBM)
    block = pltpu.VMEM((B, B, E), BF16)
    dma = pltpu.SemaphoreType.DMA
    update, hess = pl.pallas_call(
        functools.partial(kernel, sizes),
        out_shape=(jax.ShapeDtypeStruct((B, E), F32), jax.ShapeDtypeStruct((ITERS + 1, ITERS), F32)),
        in_specs=[hbm] * 10,
        out_specs=(vmem, vmem),
        scratch_shapes=[
            pltpu.VMEM((B, E), F32),
            pltpu.VMEM((FACES, E), jnp.int32),
            pltpu.VMEM((2, HALO), jnp.int32),
            block,
            block,
            block,
            pltpu.VMEM((FACES, B, B, E), BF16),
            block,
            block,
            block,
            pltpu.VMEM((2, 32 * B, E), F32),
            pltpu.VMEM((2, Q * B, LINES * B), BF16),
            pltpu.VMEM((2, HALF * B, LINES * B), BF16),
            pltpu.VMEM((Q * B, LINES * B), BF16),
            pltpu.VMEM((2, B, LINES * B), BF16),
            pltpu.VMEM((2, B, 2 * LINES * B), BF16),
            pltpu.VMEM((256, FACES * E), BF16),
            pltpu.VMEM((E, E), BF16),
            pltpu.VMEM((8, E), jnp.int32),
            pltpu.VMEM((3 + FACES, B, E), F32),
            pltpu.VMEM((B, E), F32),
            pltpu.VMEM((B, E), F32),
            pltpu.VMEM((9, B, E), F32),
            pltpu.VMEM((6, 8, E), F32),
            pltpu.VMEM((6, 3, 8, E), F32),
            pltpu.VMEM((3, B, E), BF16),
            pltpu.VMEM((3, 3, B, E), BF16),
            pltpu.VMEM((8, 8, E), F32),
            pltpu.VMEM((4, n_a, 8, E), F32),
            pltpu.VMEM((4, n_b, 8, E), F32),
            dma((10,)),
            dma((2, 2)),
            dma((2, 2)),
            dma((6, 3)),
            dma((6, 3)),
            dma((3, 3)),
            dma((3, 3)),
            dma((8,)),
            dma((8,)),
        ],
        compiler_params=pltpu.CompilerParams(
            collective_id=0, has_side_effects=True, vmem_limit_bytes=64 * 1024 * 1024
        ),
    )(right_side, nbr, send, diag, lower, upper, face, inv, fwd, bwd)
    return update, hess


def solution(mesh):
    n_dom, n_line = mesh.shape["dom"], mesh.shape["line"]
    low = 16 if n_dom >= 32 else 2
    sizes = (n_dom, n_line, n_dom // low, low)
    both = ("dom", "line")
    in_specs = (
        P(None, both),
        P(None, None, both),
        P(None, None, both),
        P(None, None, both),
        P(None, None, None, both),
        P(None, both),
        P(None, both),
        P(None, None, both),
        P(None, None, both),
        P(None, None, both),
    )
    return jax.shard_map(
        functools.partial(shards, sizes),
        mesh=mesh,
        in_specs=in_specs,
        out_specs=(P(None, both), P()),
        check_vma=False,
    )
```
